128 devices in a mesh: row: 8 (over x, z_hi), col: 16 (over y, z_lo, core).
Axes of the slice: x: 4, y: 4, z: 4 (z_hi: 2, z_lo: 2; z = z_hi * 2 + z_lo), core: 2. Of those that a mesh axis runs over, the one named last changes fastest.
Arguments:
- amplitudes: bfloat16 [16384, 512], P(('row', 'col')), may hold values from -6 to 6
- integrals: bfloat16 [512, 65536], P('row', 'col'), may hold values from -1 to 1
- pair_list: int32 [2, 16384], P(None, 'row'), may hold values from 0 to 199
- panel_order: int32 [2], replicated, may hold values from 0 to 1, each once
- occ_energy: float32 [200], replicated, may hold values from -2 to -0.4
- vir_energy: float32 [512], replicated, may hold values from 0.2 to 3
Outputs:
- update: bfloat16 [16384, 65536], P('row', 'col')
The draws below stay inside these ranges and needn't reach their ends.
Inputs may be any that keep to these rules, and one draw needn't show every extreme that they name: `panel_order`: each of the 2 panel numbers appears once.
All inputs are finite; a program needn't handle non-finite values.
Results may differ from the reference program's by a relative error of at most 0.001.
Values may be sent and summed in bfloat16 or wider, within the bound.
A program may use at most 128 MiB of HBM per device.

```python
import jax
import jax.numpy as jnp
from jax import lax

NO = 200
NV = 512
PANEL = 256
NPANEL = 2
PAIR_ROW = 2048
PAIRS = 16384
CDW = 512
AB = 65536
N_ROW = 8


def touch_ends(values, key, smallest, largest):
    shape = values.shape
    place = [jax.random.randint(jax.random.fold_in(key, axis), (), 0, shape[axis]) for axis in range(len(shape))]
    values = values.at[tuple(place)].set(smallest)
    longest = shape.index(max(shape))
    place[longest] = (place[longest] + 1) % shape[longest]
    return values.at[tuple(place)].set(largest)


def shard_levels(key, extent, pieces, smallest, largest):
    gain = 1.0
    for axis_at, shards_of in pieces:
        heights = jax.random.uniform(jax.random.fold_in(jax.random.fold_in(key, 6), axis_at), (shards_of,), jnp.float32, smallest / len(pieces), largest / len(pieces))
        gain = gain * jnp.repeat(jnp.exp(heights), extent[axis_at] // shards_of).reshape((-1,) + (1,) * (len(extent) - 1 - axis_at))
    return gain


def noise(stream_key, shape, spread, most, shards=(), held_as=jnp.bfloat16):
    factor_of = shard_levels(stream_key, shape, shards, -0.22, 0.18) if shards else 1.0
    entries = jax.random.normal(stream_key, shape, jnp.float32) * spread * factor_of
    return jnp.minimum(jnp.maximum(entries, -most), most).astype(held_as)


def setup_inputs(seed: int = 0) -> dict:
    splits = jax.random.split(jax.random.key(seed), 7)
    amplitudes = noise(splits[0], (PAIRS, CDW), 1.0, 6.0, ((0, 128),))
    integrals = noise(splits[1], (CDW, AB), (CDW // 16) ** -0.5, 1.0, ((0, 8), (1, 16)))
    pair_list = touch_ends(jax.random.randint(splits[2], (2, PAIRS), 0, NO), jax.random.fold_in(splits[2], 1), 0, NO - 1).astype(jnp.int32)
    panel_order = jax.random.permutation(splits[3], NPANEL).astype(jnp.int32)
    occ_energy = jnp.clip(jax.random.uniform(splits[4], (NO,), jnp.float32, -2.0, -0.4), -2.0, -0.4)
    vir_energy = jnp.clip(jax.random.uniform(splits[5], (NV,), jnp.float32, 0.2, 3.0), 0.2, 3.0)
    return {"amplitudes": amplitudes, "integrals": integrals, "pair_list": pair_list, "panel_order": panel_order, "occ_energy": occ_energy, "vir_energy": vir_energy}


def reference(amplitudes, integrals, pair_list, panel_order, occ_energy, vir_energy):
    blocks = [lax.dynamic_slice_in_dim(integrals, (panel_order[which] * PANEL).astype(jnp.int32), PANEL, 0) for which in range(NPANEL)]
    window = jnp.concatenate(blocks, 0)
    pair_energy = occ_energy[pair_list[0]] + occ_energy[pair_list[1]]
    columns = jnp.arange(AB)
    virt_energy = vir_energy[columns // NV] + vir_energy[columns % NV]
    amp_blocks = amplitudes.reshape(N_ROW, PAIR_ROW, CDW)
    energy_blocks = pair_energy.reshape(N_ROW, PAIR_ROW)

    def one_block(items):
        amp_block, energy_block = items
        ladder = jnp.dot(amp_block, window, preferred_element_type=jnp.float32)
        return (ladder / (energy_block[:, None] - virt_energy[None, :])).astype(jnp.bfloat16)

    result = lax.map(one_block, (amp_blocks, energy_blocks))
    return result.reshape(PAIRS, AB)
```

```python
import functools

import jax
import jax.numpy as jnp
from jax import lax
from jax.experimental import pallas as pl
from jax.experimental.pallas import tpu as pltpu
from jax.sharding import PartitionSpec as P

MESH = pl.DeviceIdType.MESH
PIECES = 8
NEAR = 5
STRIP = 512
ROWS = 64
PAIRS = 128


def ladder_tile(t_ref, w, pe_ref, ve, out):
    acc = jnp.dot(t_ref[...], w[...], preferred_element_type=jnp.float32)
    for lane in range(0, STRIP, 128):
        gap = pe_ref[...] - ve[:, lane : lane + 128]
        out[:, lane : lane + 128] = (acc[:, lane : lane + 128] / gap).astype(jnp.bfloat16)


def gather_kernel(
    ints, amps, pair_list, order_in, occ_in, vir_in, vir_row_in,
    done, t, far, pe, vir_row,
    near, amp_v, pair_v, order, occ, vir, local_sem, small_sem, w_send, w_recv, t_send, t_recv,
):
    row, col = lax.axis_index("row"), lax.axis_index("col")
    x, zh = row // 2, row % 2
    xr, xl = ((row + 2) % 8, col), ((row + 6) % 8, col)
    zz = (row + 1 - 2 * zh, col)
    yr, yl = (row, (col + 4) % 16), (row, (col + 12) % 16)
    zn = (row, col + 2 - 4 * ((col // 2) % 2))
    sib = (row, col + 1 - 2 * (col % 2))

    small = [
        pltpu.make_async_copy(here, there, small_sem.at[k])
        for k, (here, there) in enumerate((
            (amps, amp_v), (order_in, order), (pair_list, pair_v), (occ_in, occ), (vir_in, vir), (vir_row_in, vir_row),
        ))
    ]
    for copy in small:
        copy.start()

    barrier = pltpu.get_barrier_semaphore()
    for peer in (xr, xl, zz, yr, yl, zn, sib):
        pl.semaphore_signal(barrier, inc=1, device_id=peer, device_id_type=MESH)

    small[0].wait()
    small[1].wait()
    first, second = amp_v[:, 0:256], amp_v[:, 256:512]
    stored0 = jnp.full((PAIRS, 256), order[0], jnp.int32) == 0
    stored1 = jnp.full((PAIRS, 256), order[1], jnp.int32) == 1
    mine = pl.multiple_of(col * PAIRS, PAIRS)
    t[pl.ds(mine, PAIRS), 0:256] = jnp.where(stored0, first, second)
    t[pl.ds(mine, PAIRS), 256:512] = jnp.where(stored1, second, first)
    pl.semaphore_wait(barrier, 7)

    def t_rows(dy, dz, dc=0):
        zl, core = (col // 2) % 2, col % 2
        zl = zl + dz * (1 - 2 * zl)
        core = core + dc * (1 - 2 * core)
        at = ((col // 4 + dy) % 4) * 4 + zl * 2 + core
        return t.at[pl.ds(pl.multiple_of(at * PAIRS, PAIRS), PAIRS)]

    def t_copy(dy, dz, sem, peer):
        return pltpu.make_async_remote_copy(
            src_ref=t_rows(dy, dz), dst_ref=t_rows(dy, dz), send_sem=t_send, recv_sem=t_recv.at[sem],
            device_id=peer, device_id_type=MESH,
        )

    def t_wait(dy, dz, sem):
        t_copy(dy, dz, sem, sib).wait_recv()

    def w_of(p):
        return near.at[p] if p < NEAR else far.at[p - NEAR]

    def w_rows(p, dx, dz, lo=0, size=ROWS):
        at = ((x + dx) % 4) * 2 + zh + dz * (1 - 2 * zh)
        return w_of(p).at[pl.ds(pl.multiple_of(at * ROWS + lo, 32), size)]

    def w_copy(p, dx, dz, sem, peer, lo=0, size=ROWS, own=False):
        dst = w_rows(p, dx, dz, lo, size)
        src = ints.at[:, pl.ds(p * STRIP, STRIP)] if own else dst
        return pltpu.make_async_remote_copy(
            src_ref=src, dst_ref=dst, send_sem=w_send.at[p], recv_sem=w_recv.at[p, sem],
            device_id=peer, device_id_type=MESH,
        )

    def w_wait(p, dx, dz, sem):
        w_copy(p, dx, dz, sem, sib).wait_recv()

    t_copy(0, 0, 0, zn).start()
    t_copy(0, 0, 1, yr).start()
    t_copy(0, 0, 2, yl).start()
    t_copy(0, 0, 7, sib).start()
    near_ids, far_ids = list(range(NEAR)), list(range(NEAR, PIECES))
    for p in (5, 0, 6, 1, 7, 2, 3, 4):
        w_copy(p, 0, 0, 0 if p >= NEAR else 1, xr, own=True).start()
        w_copy(p, 0, 0, 1 if p >= NEAR else 3, xl, own=True).start()
        if p < NEAR:
            w_copy(p, 0, 0, 0, zz, own=True).start()
    for p in far_ids:
        w_copy(p, 0, 0, 3, zz, own=True).start()
    own_in = []
    for p in range(PIECES):
        keep = pltpu.make_async_copy(
            ints.at[:, pl.ds(p * STRIP, STRIP)], w_rows(p, 0, 0), local_sem.at[p]
        )
        keep.start()
        own_in.append(keep)

    for copy in small[2:]:
        copy.wait()
    index = pair_v[...]

    def pick(o, found):
        return jnp.where(index == o, occ[o], found)

    picked = lax.fori_loop(0, occ.shape[0], pick, jnp.zeros(index.shape, jnp.float32), unroll=8)
    pair_row = picked[0:1] + picked[1:2]
    for at in range(0, pair_row.shape[1], 128):
        spread = jnp.broadcast_to(pair_row[:, at : at + 128], (128, 128))
        pe[at : at + 128, :] = spread.T

    def near_cross(p):
        w_wait(p, 0, 1, 0)
        w_copy(p, 0, 1, 3, xr).start()
        w_copy(p, 0, 1, 2, xl).start()

    def near_right(p):
        w_wait(p, 3, 0, 1)
        w_copy(p, 3, 0, 3, xr).start()

    def near_left(p):
        w_wait(p, 1, 1, 2)
        w_copy(p, 1, 1, 3, xl).start()

    def far_spread(p):
        w_wait(p, 3, 0, 0)
        w_copy(p, 3, 0, 2, xr, 0, 32).start()
        w_copy(p, 3, 0, 3, zz).start()
        w_wait(p, 1, 0, 1)
        w_copy(p, 1, 0, 2, xl, 32, 32).start()
        w_copy(p, 1, 0, 3, zz).start()

    def far_last(p):
        w_wait(p, 2, 0, 2)
        w_copy(p, 2, 0, 3, zz).start()

    far_spread(5)
    near_cross(0)
    t_wait(0, 1, 0)
    t_copy(0, 1, 3, yr).start()
    t_copy(0, 1, 4, yl).start()
    t_copy(0, 1, 7, sib).start()
    t_wait(3, 0, 1)
    t_copy(3, 0, 5, yr).start()
    t_copy(3, 0, 7, sib).start()
    t_wait(1, 0, 2)
    t_copy(1, 0, 7, sib).start()
    near_cross(1)
    near_right(0)
    far_spread(6)
    near_cross(2)
    near_right(1)
    t_wait(1, 1, 4)
    t_copy(1, 1, 6, yl).start()
    t_copy(1, 1, 7, sib).start()
    t_wait(3, 1, 3)
    t_copy(3, 1, 7, sib).start()
    far_spread(7)
    near_cross(3)
    near_cross(4)
    near_right(2)
    near_right(3)
    near_right(4)
    t_wait(2, 0, 5)
    t_copy(2, 0, 7, sib).start()
    t_wait(2, 1, 6)
    t_copy(2, 1, 7, sib).start()
    near_left(0)
    far_last(5)
    near_left(1)
    near_left(2)
    far_last(6)
    near_left(3)
    far_last(7)
    near_left(4)

    def wait_bytes(ref, sem):
        pltpu.make_async_copy(ref, ref, sem).wait()

    wait_bytes(t.at[pl.ds(0, 8 * PAIRS)], t_recv.at[7])
    for p in near_ids:
        own_in[p].wait()
        wait_bytes(w_of(p).at[pl.ds(0, 4 * ROWS)], w_recv.at[p, 3])
        ve = vir[col * PIECES + p] + vir_row[...]
        ladder_tile(t, w_of(p), pe, ve, done.at[:, pl.ds(p * STRIP, STRIP)])
    for p in far_ids:
        own_in[p].wait()
        wait_bytes(w_of(p).at[pl.ds(0, 4 * ROWS)], w_recv.at[p, 3])
    for p in range(PIECES):
        wait_bytes(w_of(p).at[pl.ds(0, 7 * ROWS)], w_send.at[p])
    wait_bytes(t.at[pl.ds(0, 15 * PAIRS)], t_send)


def finish_kernel(done, t, far, pe, vir_row, vir_in, out, tail, vir, vir_sem, sem):
    col = lax.axis_index("col")
    width = NEAR * STRIP
    copies = [pltpu.make_async_copy(done, out.at[:, pl.ds(0, width)], sem.at[0])]
    copies[0].start()
    vir_copy = pltpu.make_async_copy(vir_in, vir, vir_sem)
    vir_copy.start()
    vir_copy.wait()
    for k in range(PIECES - NEAR):
        ve = vir[col * PIECES + NEAR + k] + vir_row[...]
        ladder_tile(t, far.at[k], pe, ve, tail.at[k])
        copy = pltpu.make_async_copy(
            tail.at[k], out.at[:, pl.ds(width + k * STRIP, STRIP)], sem.at[k + 1]
        )
        copy.start()
        copies.append(copy)
    for copy in copies:
        copy.wait()


def shards(amplitudes, integrals, pair_list, panel_order, occ_energy, vir_energy):
    vmem, hbm = pl.BlockSpec(memory_space=pltpu.VMEM), pl.BlockSpec(memory_space=pltpu.HBM)
    rows, depth, columns = 16 * PAIRS, 8 * ROWS, PIECES * STRIP
    far_count = PIECES - NEAR
    done, t, far, pe, vir_row = pl.pallas_call(
        gather_kernel,
        out_shape=(
            pltpu.VMEM((rows, NEAR * STRIP), jnp.bfloat16),
            pltpu.VMEM((rows, depth), jnp.bfloat16),
            pltpu.VMEM((far_count, depth, STRIP), jnp.bfloat16),
            pltpu.VMEM((rows, 128), jnp.float32),
            pltpu.VMEM((1, vir_energy.shape[0]), jnp.float32),
        ),
        in_specs=[hbm] * 7,
        out_specs=(vmem,) * 5,
        scratch_shapes=[
            pltpu.VMEM((NEAR, depth, STRIP), jnp.bfloat16),
            pltpu.VMEM((PAIRS, depth), jnp.bfloat16),
            pltpu.VMEM((2, rows), jnp.int32),
            pltpu.SMEM((2,), jnp.int32),
            pltpu.SMEM((200,), jnp.float32),
            pltpu.SMEM((512,), jnp.float32),
            pltpu.SemaphoreType.DMA((PIECES,)),
            pltpu.SemaphoreType.DMA((6,)),
            pltpu.SemaphoreType.DMA((PIECES,)),
            pltpu.SemaphoreType.DMA((PIECES, 4)),
            pltpu.SemaphoreType.DMA,
            pltpu.SemaphoreType.DMA((8,)),
        ],
        cost_estimate=pl.CostEstimate(
            flops=2 * rows * depth * NEAR * STRIP, bytes_accessed=4 << 20, transcendentals=0
        ),
        compiler_params=pltpu.CompilerParams(
            collective_id=0, has_side_effects=True, vmem_limit_bytes=32 << 20
        ),
        name="gather",
    )(*(pltpu.with_memory_space_constraint(given, pltpu.HBM) for given in (
        integrals, amplitudes, pair_list, panel_order, occ_energy, vir_energy, vir_energy.reshape(1, -1),
    )))
    return pl.pallas_call(
        finish_kernel,
        out_shape=jax.ShapeDtypeStruct((rows, columns), jnp.bfloat16),
        in_specs=[vmem] * 5 + [hbm],
        out_specs=hbm,
        scratch_shapes=[
            pltpu.VMEM((far_count, rows, STRIP), jnp.bfloat16),
            pltpu.SMEM((512,), jnp.float32),
            pltpu.SemaphoreType.DMA,
            pltpu.SemaphoreType.DMA((far_count + 1,)),
        ],
        cost_estimate=pl.CostEstimate(
            flops=2 * rows * depth * far_count * STRIP,
            bytes_accessed=2 * rows * columns,
            transcendentals=0,
        ),
        compiler_params=pltpu.CompilerParams(vmem_limit_bytes=32 << 20),
        name="finish",
    )(done, t, far, pe, vir_row, pltpu.with_memory_space_constraint(vir_energy, pltpu.HBM))


def solution(mesh):
    placed = (P(("row", "col"), None), P("row", "col"), P(None, "row"), P(), P(), P())
    return jax.shard_map(
        shards, mesh=mesh, in_specs=placed, out_specs=P("row", "col"), check_vma=False
    )
```

```python
import functools

import jax
import jax.numpy as jnp
from jax import lax
from jax.experimental import pallas as pl
from jax.experimental.pallas import tpu as pltpu
from jax.sharding import PartitionSpec as P

MESH = pl.DeviceIdType.MESH
PIECES = 8
EARLY = 5
FAR = (1, 3, 7)
STRIP = 512
ROWS = 64
PAIRS = 128

STEPS = (
    ("ox", 1), ("oz", 4), ("oz", 2), ("ox", 7), ("ox", 5), ("oz", 0), ("pairs", 0), ("t00", 0), ("oz", 5), ("fl", 1),
    ("ox", 3), ("ox", 0), ("fr", 1), ("nc", 2), ("t30", 0), ("ox", 6), ("fr", 3), ("nr", 0), ("t20", 0), ("t01", 0),
    ("oz", 6), ("fl", 3), ("oz", 1), ("ox", 2), ("t10", 0), ("nc", 0), ("ox", 4), ("ff", 1), ("oz", 3), ("t31", 0),
    ("ff", 3), ("t11", 0), ("fr", 7), ("nc", 4), ("nr", 2), ("nl", 0), ("fl", 7), ("nr", 4), ("nr", 5), ("nc", 5),
    ("t21", 0), ("nl", 2), ("nc", 6), ("oz", 7), ("nr", 6), ("ff", 7), ("mul", 0), ("nl", 4), ("nl", 5), ("mul", 1),
    ("nl", 6), ("mul", 2), ("mul", 3), ("mul", 4),
)


def ladder_tile(t_ref, w, pe_ref, ve, out):
    acc = jnp.dot(t_ref[...], w[...], preferred_element_type=jnp.float32)
    for lane in range(0, STRIP, 128):
        gap = pe_ref[...] - ve[:, lane : lane + 128]
        out[:, lane : lane + 128] = (acc[:, lane : lane + 128] / gap).astype(jnp.bfloat16)


def gather_kernel(
    ints, amps, pair_list, order_in, occ_in, vir_in, vir_row_in,
    done, t, late, pe, vir_row,
    early, amp_v, pair_v, order, occ, vir, local_sem, small_sem, w_send, w_recv, t_send, t_recv,
):
    row, col = lax.axis_index("row"), lax.axis_index("col")
    x, zh = row // 2, row % 2
    xr, xl = ((row + 2) % 8, col), ((row + 6) % 8, col)
    zz = (row + 1 - 2 * zh, col)
    yr, yl = (row, (col + 4) % 16), (row, (col + 12) % 16)
    zn = (row, col + 2 - 4 * ((col // 2) % 2))
    sib = (row, col + 1 - 2 * (col % 2))

    small = [
        pltpu.make_async_copy(here, there, small_sem.at[k])
        for k, (here, there) in enumerate((
            (amps, amp_v), (order_in, order), (pair_list, pair_v), (occ_in, occ), (vir_in, vir), (vir_row_in, vir_row),
        ))
    ]
    for copy in small:
        copy.start()

    barrier = pltpu.get_barrier_semaphore()
    for peer in (xr, xl, zz, yr, yl, zn, sib):
        pl.semaphore_signal(barrier, inc=1, device_id=peer, device_id_type=MESH)

    pl.semaphore_wait(barrier, 7)

    def t_rows(dy, dz, dc=0):
        zl, core = (col // 2) % 2, col % 2
        zl = zl + dz * (1 - 2 * zl)
        core = core + dc * (1 - 2 * core)
        at = ((col // 4 + dy) % 4) * 4 + zl * 2 + core
        return t.at[pl.ds(pl.multiple_of(at * PAIRS, PAIRS), PAIRS)]

    def t_copy(dy, dz, sem, peer):
        return pltpu.make_async_remote_copy(
            src_ref=t_rows(dy, dz), dst_ref=t_rows(dy, dz), send_sem=t_send, recv_sem=t_recv.at[sem],
            device_id=peer, device_id_type=MESH,
        )

    def t_wait(dy, dz, sem):
        t_copy(dy, dz, sem, sib).wait_recv()

    def w_of(p):
        return early.at[p] if p < EARLY else late.at[p - EARLY]

    def w_rows(p, dx, dz, lo=0, size=ROWS):
        at = ((x + dx) % 4) * 2 + zh + dz * (1 - 2 * zh)
        return w_of(p).at[pl.ds(pl.multiple_of(at * ROWS + lo, 32), size)]

    def w_copy(p, dx, dz, sem, peer, lo=0, size=ROWS, own=False):
        dst = w_rows(p, dx, dz, lo, size)
        src = ints.at[:, pl.ds(p * STRIP, STRIP)] if own else dst
        return pltpu.make_async_remote_copy(
            src_ref=src, dst_ref=dst, send_sem=w_send.at[p], recv_sem=w_recv.at[p, sem],
            device_id=peer, device_id_type=MESH,
        )

    def w_wait(p, dx, dz, sem):
        w_copy(p, dx, dz, sem, sib).wait_recv()

    own_in = []
    for p in range(PIECES):
        own_in.append(
            pltpu.make_async_copy(ints.at[:, pl.ds(p * STRIP, STRIP)], w_rows(p, 0, 0), local_sem.at[p])
        )

    def ox(p):
        w_copy(p, 0, 0, 0 if p in FAR else 1, xr, own=True).start()
        w_copy(p, 0, 0, 1 if p in FAR else 3, xl, own=True).start()

    def oz(p):
        w_copy(p, 0, 0, 3 if p in FAR else 0, zz, own=True).start()
        own_in[p].start()

    def nc(p):
        w_wait(p, 0, 1, 0)
        w_copy(p, 0, 1, 3, xr).start()
        w_copy(p, 0, 1, 2, xl).start()

    def nr(p):
        w_wait(p, 3, 0, 1)
        w_copy(p, 3, 0, 3, xr).start()

    def nl(p):
        w_wait(p, 1, 1, 2)
        w_copy(p, 1, 1, 3, xl).start()

    def fr(p):
        w_wait(p, 3, 0, 0)
        w_copy(p, 3, 0, 2, xr, 0, 32).start()
        w_copy(p, 3, 0, 3, zz).start()

    def fl(p):
        w_wait(p, 1, 0, 1)
        w_copy(p, 1, 0, 2, xl, 32, 32).start()
        w_copy(p, 1, 0, 3, zz).start()

    def ff(p):
        w_wait(p, 2, 0, 2)
        w_copy(p, 2, 0, 3, zz).start()

    def t00(_):
        small[0].wait()
        small[1].wait()
        first, second = amp_v[:, 0:256], amp_v[:, 256:512]
        stored0 = jnp.full((PAIRS, 256), order[0], jnp.int32) == 0
        stored1 = jnp.full((PAIRS, 256), order[1], jnp.int32) == 1
        mine = pl.multiple_of(col * PAIRS, PAIRS)
        t[pl.ds(mine, PAIRS), 0:256] = jnp.where(stored0, first, second)
        t[pl.ds(mine, PAIRS), 256:512] = jnp.where(stored1, second, first)
        t_copy(0, 0, 0, zn).start()
        t_copy(0, 0, 1, yr).start()
        t_copy(0, 0, 2, yl).start()
        t_copy(0, 0, 7, sib).start()

    def t01(_):
        t_wait(0, 1, 0)
        t_copy(0, 1, 3, yr).start()
        t_copy(0, 1, 4, yl).start()
        t_copy(0, 1, 7, sib).start()

    def t30(_):
        t_wait(3, 0, 1)
        t_copy(3, 0, 5, yr).start()
        t_copy(3, 0, 7, sib).start()

    def t10(_):
        t_wait(1, 0, 2)
        t_copy(1, 0, 7, sib).start()

    def t31(_):
        t_wait(3, 1, 3)
        t_copy(3, 1, 7, sib).start()

    def t11(_):
        t_wait(1, 1, 4)
        t_copy(1, 1, 6, yl).start()
        t_copy(1, 1, 7, sib).start()

    def t20(_):
        t_wait(2, 0, 5)
        t_copy(2, 0, 7, sib).start()

    def t21(_):
        t_wait(2, 1, 6)
        t_copy(2, 1, 7, sib).start()

    def pairs(_):
        for copy in small[2:]:
            copy.wait()
        index = pair_v[...]

        def pick(o, found):
            return jnp.where(index == o, occ[o], found)

        picked = lax.fori_loop(0, occ.shape[0], pick, jnp.zeros(index.shape, jnp.float32), unroll=8)
        pair_row = picked[0:1] + picked[1:2]
        for at in range(0, pair_row.shape[1], 128):
            spread = jnp.broadcast_to(pair_row[:, at : at + 128], (128, 128))
            pe[at : at + 128, :] = spread.T

    def wait_bytes(ref, sem):
        pltpu.make_async_copy(ref, ref, sem).wait()

    def whole(p):
        own_in[p].wait()
        wait_bytes(w_of(p).at[pl.ds(0, 4 * ROWS)], w_recv.at[p, 3])

    def mul(p):
        if p == 0:
            wait_bytes(t.at[pl.ds(0, 8 * PAIRS)], t_recv.at[7])
        whole(p)
        ve = vir[col * PIECES + p] + vir_row[...]
        ladder_tile(t, w_of(p), pe, ve, done.at[:, pl.ds(p * STRIP, STRIP)])

    steps = dict(
        ox=ox, oz=oz, nc=nc, nr=nr, nl=nl, fr=fr, fl=fl, ff=ff, mul=mul, pairs=pairs,
        t00=t00, t01=t01, t30=t30, t10=t10, t31=t31, t11=t11, t20=t20, t21=t21,
    )
    for name, p in STEPS:
        steps[name](p)
    for p in range(EARLY, PIECES):
        whole(p)
    for p in range(PIECES):
        wait_bytes(w_of(p).at[pl.ds(0, 7 * ROWS)], w_send.at[p])
    wait_bytes(t.at[pl.ds(0, 15 * PAIRS)], t_send)


def finish_kernel(done, t, late, pe, vir_row, vir_in, out, tail, vir, vir_sem, sem):
    col = lax.axis_index("col")
    width = EARLY * STRIP
    copies = [pltpu.make_async_copy(done, out.at[:, pl.ds(0, width)], sem.at[0])]
    copies[0].start()
    vir_copy = pltpu.make_async_copy(vir_in, vir, vir_sem)
    vir_copy.start()
    vir_copy.wait()
    for k in range(PIECES - EARLY):
        ve = vir[col * PIECES + EARLY + k] + vir_row[...]
        ladder_tile(t, late.at[k], pe, ve, tail.at[k])
        copy = pltpu.make_async_copy(
            tail.at[k], out.at[:, pl.ds(width + k * STRIP, STRIP)], sem.at[k + 1]
        )
        copy.start()
        copies.append(copy)
    for copy in copies:
        copy.wait()


def shards(amplitudes, integrals, pair_list, panel_order, occ_energy, vir_energy):
    vmem, hbm = pl.BlockSpec(memory_space=pltpu.VMEM), pl.BlockSpec(memory_space=pltpu.HBM)
    rows, depth, columns = 16 * PAIRS, 8 * ROWS, PIECES * STRIP
    late_count = PIECES - EARLY
    done, t, late, pe, vir_row = pl.pallas_call(
        gather_kernel,
        out_shape=(
            pltpu.VMEM((rows, EARLY * STRIP), jnp.bfloat16),
            pltpu.VMEM((rows, depth), jnp.bfloat16),
            pltpu.VMEM((late_count, depth, STRIP), jnp.bfloat16),
            pltpu.VMEM((rows, 128), jnp.float32),
            pltpu.VMEM((1, vir_energy.shape[0]), jnp.float32),
        ),
        in_specs=[hbm] * 7,
        out_specs=(vmem,) * 5,
        scratch_shapes=[
            pltpu.VMEM((EARLY, depth, STRIP), jnp.bfloat16),
            pltpu.VMEM((PAIRS, depth), jnp.bfloat16),
            pltpu.VMEM((2, rows), jnp.int32),
            pltpu.SMEM((2,), jnp.int32),
            pltpu.SMEM((200,), jnp.float32),
            pltpu.SMEM((512,), jnp.float32),
            pltpu.SemaphoreType.DMA((PIECES,)),
            pltpu.SemaphoreType.DMA((6,)),
            pltpu.SemaphoreType.DMA((PIECES,)),
            pltpu.SemaphoreType.DMA((PIECES, 4)),
            pltpu.SemaphoreType.DMA,
            pltpu.SemaphoreType.DMA((8,)),
        ],
        cost_estimate=pl.CostEstimate(
            flops=2 * rows * depth * EARLY * STRIP, bytes_accessed=4 << 20, transcendentals=0
        ),
        compiler_params=pltpu.CompilerParams(
            collective_id=0, has_side_effects=True, vmem_limit_bytes=32 << 20
        ),
        name="gather",
    )(*(pltpu.with_memory_space_constraint(given, pltpu.HBM) for given in (
        integrals, amplitudes, pair_list, panel_order, occ_energy, vir_energy, vir_energy.reshape(1, -1),
    )))
    return pl.pallas_call(
        finish_kernel,
        out_shape=jax.ShapeDtypeStruct((rows, columns), jnp.bfloat16),
        in_specs=[vmem] * 5 + [hbm],
        out_specs=hbm,
        scratch_shapes=[
            pltpu.VMEM((late_count, rows, STRIP), jnp.bfloat16),
            pltpu.SMEM((512,), jnp.float32),
            pltpu.SemaphoreType.DMA,
            pltpu.SemaphoreType.DMA((late_count + 1,)),
        ],
        cost_estimate=pl.CostEstimate(
            flops=2 * rows * depth * late_count * STRIP,
            bytes_accessed=2 * rows * columns,
            transcendentals=0,
        ),
        compiler_params=pltpu.CompilerParams(vmem_limit_bytes=32 << 20),
        name="finish",
    )(done, t, late, pe, vir_row, pltpu.with_memory_space_constraint(vir_energy, pltpu.HBM))


def solution(mesh):
    placed = (P(("row", "col"), None), P("row", "col"), P(None, "row"), P(), P(), P())
    return jax.shard_map(
        shards, mesh=mesh, in_specs=placed, out_specs=P("row", "col"), check_vma=False
    )
```

```python
import functools

import jax
import jax.numpy as jnp
from jax import lax
from jax.experimental import pallas as pl
from jax.experimental.pallas import tpu as pltpu
from jax.sharding import PartitionSpec as P

MESH = pl.DeviceIdType.MESH
PIECES = 8
EARLY = 5
FAR = (1, 3, 7)
STRIP = 512
ROWS = 64
PAIRS = 128

STEPS = (
    ("ox", 1), ("oz", 4), ("oz", 2), ("ox", 7), ("ox", 5), ("oz", 0), ("pairs", 0), ("t00", 0), ("oz", 5), ("fl", 1),
    ("ox", 3), ("ox", 0), ("fr", 1), ("nc", 2), ("t30", 0), ("ox", 6), ("fr", 3), ("nr", 0), ("t20", 0), ("t01", 0),
    ("oz", 6), ("fl", 3), ("oz", 1), ("ox", 2), ("t10", 0), ("nc", 0), ("ox", 4), ("ff", 1), ("oz", 3), ("t31", 0),
    ("ff", 3), ("t11", 0), ("fr", 7), ("nc", 4), ("nr", 2), ("nl", 0), ("fl", 7), ("nr", 4), ("nr", 5), ("nc", 5),
    ("t21", 0), ("nl", 2), ("nc", 6), ("oz", 7), ("nr", 6), ("ff", 7), ("mul", 0), ("nl", 4), ("nl", 5), ("mul", 1),
    ("nl", 6), ("mul", 2), ("mul", 3), ("mul", 4),
)


def ladder_tile(t_ref, w, pe_ref, ve, out):
    acc = jnp.dot(t_ref[...], w[...], preferred_element_type=jnp.float32)
    for lane in range(0, STRIP, 128):
        gap = pe_ref[...] - ve[:, lane : lane + 128]
        out[:, lane : lane + 128] = (acc[:, lane : lane + 128] / gap).astype(jnp.bfloat16)


def gather_kernel(
    ints, amps, pair_list, order_in, occ_in, vir_in, vir_row_in,
    done, t, late, pe, late_ve,
    early, amp_v, pair_v, vir_row, order, occ, vir, local_sem, small_sem, w_send, w_recv, t_send, t_recv,
):
    row, col = lax.axis_index("row"), lax.axis_index("col")
    x, zh = row // 2, row % 2
    xr, xl = ((row + 2) % 8, col), ((row + 6) % 8, col)
    zz = (row + 1 - 2 * zh, col)
    yr, yl = (row, (col + 4) % 16), (row, (col + 12) % 16)
    zn = (row, col + 2 - 4 * ((col // 2) % 2))
    sib = (row, col + 1 - 2 * (col % 2))

    barrier = pltpu.get_barrier_semaphore()
    for peer in (xr, xl, zz, yr, yl, zn, sib):
        pl.semaphore_signal(barrier, inc=1, device_id=peer, device_id_type=MESH)

    small = [
        pltpu.make_async_copy(here, there, small_sem.at[k])
        for k, (here, there) in enumerate((
            (amps, amp_v), (order_in, order), (pair_list, pair_v), (occ_in, occ), (vir_in, vir), (vir_row_in, vir_row),
        ))
    ]
    for copy in small:
        copy.start()

    pl.semaphore_wait(barrier, 7)

    def t_rows(dy, dz, dc=0):
        zl, core = (col // 2) % 2, col % 2
        zl = zl + dz * (1 - 2 * zl)
        core = core + dc * (1 - 2 * core)
        at = ((col // 4 + dy) % 4) * 4 + zl * 2 + core
        return t.at[pl.ds(pl.multiple_of(at * PAIRS, PAIRS), PAIRS)]

    def t_copy(dy, dz, sem, peer):
        return pltpu.make_async_remote_copy(
            src_ref=t_rows(dy, dz), dst_ref=t_rows(dy, dz), send_sem=t_send, recv_sem=t_recv.at[sem],
            device_id=peer, device_id_type=MESH,
        )

    def t_wait(dy, dz, sem):
        t_copy(dy, dz, sem, sib).wait_recv()

    def w_of(p):
        return early.at[p] if p < EARLY else late.at[p - EARLY]

    def w_rows(p, dx, dz, lo=0, size=ROWS):
        at = ((x + dx) % 4) * 2 + zh + dz * (1 - 2 * zh)
        return w_of(p).at[pl.ds(pl.multiple_of(at * ROWS + lo, 32), size)]

    def w_copy(p, dx, dz, sem, peer, lo=0, size=ROWS, own=False):
        dst = w_rows(p, dx, dz, lo, size)
        src = ints.at[:, pl.ds(p * STRIP, STRIP)] if own else dst
        return pltpu.make_async_remote_copy(
            src_ref=src, dst_ref=dst, send_sem=w_send.at[p], recv_sem=w_recv.at[p, sem],
            device_id=peer, device_id_type=MESH,
        )

    def w_wait(p, dx, dz, sem):
        w_copy(p, dx, dz, sem, sib).wait_recv()

    own_in = []
    for p in range(PIECES):
        own_in.append(
            pltpu.make_async_copy(ints.at[:, pl.ds(p * STRIP, STRIP)], w_rows(p, 0, 0), local_sem.at[p])
        )

    def ox(p):
        w_copy(p, 0, 0, 0 if p in FAR else 1, xr, own=True).start()
        w_copy(p, 0, 0, 1 if p in FAR else 3, xl, own=True).start()

    def oz(p):
        w_copy(p, 0, 0, 3 if p in FAR else 0, zz, own=True).start()
        own_in[p].start()

    def nc(p):
        w_wait(p, 0, 1, 0)
        w_copy(p, 0, 1, 3, xr).start()
        w_copy(p, 0, 1, 2, xl).start()

    def nr(p):
        w_wait(p, 3, 0, 1)
        w_copy(p, 3, 0, 3, xr).start()

    def nl(p):
        w_wait(p, 1, 1, 2)
        w_copy(p, 1, 1, 3, xl).start()

    def fr(p):
        w_wait(p, 3, 0, 0)
        w_copy(p, 3, 0, 2, xr, 0, 32).start()
        w_copy(p, 3, 0, 3, zz).start()

    def fl(p):
        w_wait(p, 1, 0, 1)
        w_copy(p, 1, 0, 2, xl, 32, 32).start()
        w_copy(p, 1, 0, 3, zz).start()

    def ff(p):
        w_wait(p, 2, 0, 2)
        w_copy(p, 2, 0, 3, zz).start()

    def t00(_):
        small[0].wait()
        small[1].wait()
        first, second = amp_v[:, 0:256], amp_v[:, 256:512]
        stored0 = jnp.full((PAIRS, 256), order[0], jnp.int32) == 0
        stored1 = jnp.full((PAIRS, 256), order[1], jnp.int32) == 1
        mine = pl.multiple_of(col * PAIRS, PAIRS)
        t[pl.ds(mine, PAIRS), 0:256] = jnp.where(stored0, first, second)
        t[pl.ds(mine, PAIRS), 256:512] = jnp.where(stored1, second, first)
        t_copy(0, 0, 0, zn).start()
        t_copy(0, 0, 1, yr).start()
        t_copy(0, 0, 2, yl).start()
        t_copy(0, 0, 7, sib).start()

    def t01(_):
        t_wait(0, 1, 0)
        t_copy(0, 1, 3, yr).start()
        t_copy(0, 1, 4, yl).start()
        t_copy(0, 1, 7, sib).start()

    def t30(_):
        t_wait(3, 0, 1)
        t_copy(3, 0, 5, yr).start()
        t_copy(3, 0, 7, sib).start()

    def t10(_):
        t_wait(1, 0, 2)
        t_copy(1, 0, 7, sib).start()

    def t31(_):
        t_wait(3, 1, 3)
        t_copy(3, 1, 7, sib).start()

    def t11(_):
        t_wait(1, 1, 4)
        t_copy(1, 1, 6, yl).start()
        t_copy(1, 1, 7, sib).start()

    def t20(_):
        t_wait(2, 0, 5)
        t_copy(2, 0, 7, sib).start()

    def t21(_):
        t_wait(2, 1, 6)
        t_copy(2, 1, 7, sib).start()

    def pairs(_):
        for copy in small[2:]:
            copy.wait()
        index = pair_v[...]

        def pick(o, found):
            return jnp.where(index == o, occ[o], found)

        picked = lax.fori_loop(0, occ.shape[0], pick, jnp.zeros(index.shape, jnp.float32), unroll=8)
        pair_row = picked[0:1] + picked[1:2]
        for at in range(0, pair_row.shape[1], 128):
            spread = jnp.broadcast_to(pair_row[:, at : at + 128], (128, 128))
            pe[at : at + 128, :] = spread.T
        for p in range(EARLY, PIECES):
            late_ve[:, (p - EARLY) * STRIP : (p - EARLY + 1) * STRIP] = vir[col * PIECES + p] + vir_row[...]

    def wait_bytes(ref, sem):
        pltpu.make_async_copy(ref, ref, sem).wait()

    def whole(p):
        own_in[p].wait()
        wait_bytes(w_of(p).at[pl.ds(0, 4 * ROWS)], w_recv.at[p, 3])

    def mul(p):
        if p == 0:
            wait_bytes(t.at[pl.ds(0, 8 * PAIRS)], t_recv.at[7])
        whole(p)
        ve = vir[col * PIECES + p] + vir_row[...]
        ladder_tile(t, w_of(p), pe, ve, done.at[:, pl.ds(p * STRIP, STRIP)])

    steps = dict(
        ox=ox, oz=oz, nc=nc, nr=nr, nl=nl, fr=fr, fl=fl, ff=ff, mul=mul, pairs=pairs,
        t00=t00, t01=t01, t30=t30, t10=t10, t31=t31, t11=t11, t20=t20, t21=t21,
    )
    for name, p in STEPS:
        steps[name](p)
    wait_bytes(t.at[pl.ds(0, 15 * PAIRS)], t_send)
    for p in range(PIECES):
        wait_bytes(w_of(p).at[pl.ds(0, 7 * ROWS)], w_send.at[p])
    for p in range(EARLY, PIECES):
        whole(p)


def finish_kernel(done, t, late, pe, late_ve, out, tail, sem):
    width = EARLY * STRIP
    copies = [pltpu.make_async_copy(done, out.at[:, pl.ds(0, width)], sem.at[0])]
    copies[0].start()
    for k in range(PIECES - EARLY):
        ladder_tile(t, late.at[k], pe, late_ve[:, k * STRIP : (k + 1) * STRIP], tail.at[k])
        copy = pltpu.make_async_copy(
            tail.at[k], out.at[:, pl.ds(width + k * STRIP, STRIP)], sem.at[k + 1]
        )
        copy.start()
        copies.append(copy)
    for copy in copies:
        copy.wait()


def shards(amplitudes, integrals, pair_list, panel_order, occ_energy, vir_energy):
    vmem, hbm = pl.BlockSpec(memory_space=pltpu.VMEM), pl.BlockSpec(memory_space=pltpu.HBM)
    rows, depth, columns = 16 * PAIRS, 8 * ROWS, PIECES * STRIP
    late_count = PIECES - EARLY
    done, t, late, pe, late_ve = pl.pallas_call(
        gather_kernel,
        out_shape=(
            pltpu.VMEM((rows, EARLY * STRIP), jnp.bfloat16),
            pltpu.VMEM((rows, depth), jnp.bfloat16),
            pltpu.VMEM((late_count, depth, STRIP), jnp.bfloat16),
            pltpu.VMEM((rows, 128), jnp.float32),
            pltpu.VMEM((1, late_count * STRIP), jnp.float32),
        ),
        in_specs=[hbm] * 7,
        out_specs=(vmem,) * 5,
        scratch_shapes=[
            pltpu.VMEM((EARLY, depth, STRIP), jnp.bfloat16),
            pltpu.VMEM((PAIRS, depth), jnp.bfloat16),
            pltpu.VMEM((2, rows), jnp.int32),
            pltpu.VMEM((1, vir_energy.shape[0]), jnp.float32),
            pltpu.SMEM((2,), jnp.int32),
            pltpu.SMEM((200,), jnp.float32),
            pltpu.SMEM((512,), jnp.float32),
            pltpu.SemaphoreType.DMA((PIECES,)),
            pltpu.SemaphoreType.DMA((6,)),
            pltpu.SemaphoreType.DMA((PIECES,)),
            pltpu.SemaphoreType.DMA((PIECES, 4)),
            pltpu.SemaphoreType.DMA,
            pltpu.SemaphoreType.DMA((8,)),
        ],
        cost_estimate=pl.CostEstimate(
            flops=2 * rows * depth * EARLY * STRIP, bytes_accessed=4 << 20, transcendentals=0
        ),
        compiler_params=pltpu.CompilerParams(
            collective_id=0, has_side_effects=True, vmem_limit_bytes=32 << 20
        ),
        name="gather",
    )(*(pltpu.with_memory_space_constraint(given, pltpu.HBM) for given in (
        integrals, amplitudes, pair_list, panel_order, occ_energy, vir_energy, vir_energy.reshape(1, -1),
    )))
    return pl.pallas_call(
        finish_kernel,
        out_shape=jax.ShapeDtypeStruct((rows, columns), jnp.bfloat16),
        in_specs=[vmem] * 5,
        out_specs=hbm,
        scratch_shapes=[
            pltpu.VMEM((late_count, rows, STRIP), jnp.bfloat16),
            pltpu.SemaphoreType.DMA((late_count + 1,)),
        ],
        cost_estimate=pl.CostEstimate(
            flops=2 * rows * depth * late_count * STRIP,
            bytes_accessed=2 * rows * columns,
            transcendentals=0,
        ),
        compiler_params=pltpu.CompilerParams(vmem_limit_bytes=32 << 20),
        name="finish",
    )(done, t, late, pe, late_ve)


def solution(mesh):
    placed = (P(("row", "col"), None), P("row", "col"), P(None, "row"), P(), P(), P())
    return jax.shard_map(
        shards, mesh=mesh, in_specs=placed, out_specs=P("row", "col"), check_vma=False
    )
```

```python
import functools

import jax
import jax.numpy as jnp
from jax import lax
from jax.experimental import pallas as pl
from jax.experimental.pallas import tpu as pltpu
from jax.sharding import PartitionSpec as P

MESH = pl.DeviceIdType.MESH
PIECES = 8
EARLY = 5
FAR = (1, 3, 7)
STRIP = 512
ROWS = 64
PAIRS = 128

STEPS = (
    ("ox", 1), ("oz", 4), ("oz", 2), ("ox", 7), ("ox", 5), ("oz", 0), ("pairs", 0), ("t00", 0), ("oz", 5), ("fl", 1),
    ("ox", 3), ("ox", 0), ("fr", 1), ("nc", 2), ("t30", 0), ("ox", 6), ("fr", 3), ("nr", 0), ("t20", 0), ("t01", 0),
    ("oz", 6), ("fl", 3), ("oz", 1), ("ox", 2), ("t10", 0), ("nc", 0), ("ox", 4), ("ff", 1), ("oz", 3), ("t31", 0),
    ("ff", 3), ("t11", 0), ("fr", 7), ("nc", 4), ("nr", 2), ("nl", 0), ("fl", 7), ("nr", 4), ("nr", 5), ("nc", 5),
    ("t21", 0), ("nl", 2), ("nc", 6), ("oz", 7), ("nr", 6), ("ff", 7), ("mul", 0), ("nl", 4), ("nl", 5), ("mul", 1),
    ("nl", 6), ("mul", 2), ("mul", 3), ("mul", 4),
)


def ladder_tile(t_ref, w, pe_ref, ve, out):
    acc = jnp.dot(t_ref[...], w[...], preferred_element_type=jnp.float32)
    for lane in range(0, STRIP, 128):
        gap = pe_ref[...] - ve[:, lane : lane + 128]
        out[:, lane : lane + 128] = (acc[:, lane : lane + 128] / gap).astype(jnp.bfloat16)


def gather_kernel(
    ints, amps, pair_list, order_in, occ_in, vir_in, vir_row_in,
    done, t, late, pe, late_ve,
    early, amp_v, pair_v, vir_row, order, occ, vir, local_sem, small_sem, w_send, w_recv, t_send, t_recv,
):
    row, col = lax.axis_index("row"), lax.axis_index("col")
    x, zh = row // 2, row % 2
    xr, xl = ((row + 2) % 8, col), ((row + 6) % 8, col)
    zz = (row + 1 - 2 * zh, col)
    yr, yl = (row, (col + 4) % 16), (row, (col + 12) % 16)
    zn = (row, col + 2 - 4 * ((col // 2) % 2))
    sib = (row, col + 1 - 2 * (col % 2))

    barrier = pltpu.get_barrier_semaphore()
    for peer in (xr, xl, zz, yr, yl, zn, sib):
        pl.semaphore_signal(barrier, inc=1, device_id=peer, device_id_type=MESH)

    small = [
        pltpu.make_async_copy(here, there, small_sem.at[k])
        for k, (here, there) in enumerate((
            (amps, amp_v), (order_in, order), (pair_list, pair_v), (occ_in, occ), (vir_in, vir), (vir_row_in, vir_row),
        ))
    ]
    for copy in small:
        copy.start()

    def t_rows(dy, dz, dc=0):
        zl, core = (col // 2) % 2, col % 2
        zl = zl + dz * (1 - 2 * zl)
        core = core + dc * (1 - 2 * core)
        at = ((col // 4 + dy) % 4) * 4 + zl * 2 + core
        return t.at[pl.ds(pl.multiple_of(at * PAIRS, PAIRS), PAIRS)]

    def t_copy(dy, dz, sem, peer):
        return pltpu.make_async_remote_copy(
            src_ref=t_rows(dy, dz), dst_ref=t_rows(dy, dz), send_sem=t_send, recv_sem=t_recv.at[sem],
            device_id=peer, device_id_type=MESH,
        )

    def t_wait(dy, dz, sem):
        t_copy(dy, dz, sem, sib).wait_recv()

    def w_of(p):
        return early.at[p] if p < EARLY else late.at[p - EARLY]

    def w_rows(p, dx, dz, lo=0, size=ROWS):
        at = ((x + dx) % 4) * 2 + zh + dz * (1 - 2 * zh)
        return w_of(p).at[pl.ds(pl.multiple_of(at * ROWS + lo, 32), size)]

    def w_copy(p, dx, dz, sem, peer, lo=0, size=ROWS):
        block = w_rows(p, dx, dz, lo, size)
        return pltpu.make_async_remote_copy(
            src_ref=block, dst_ref=block, send_sem=w_send.at[p], recv_sem=w_recv.at[p, sem],
            device_id=peer, device_id_type=MESH,
        )

    def w_wait(p, dx, dz, sem):
        w_copy(p, dx, dz, sem, sib).wait_recv()

    own_in = []
    for p in range(PIECES):
        copy = pltpu.make_async_copy(ints.at[:, pl.ds(p * STRIP, STRIP)], w_rows(p, 0, 0), local_sem.at[p])
        copy.start()
        own_in.append(copy)
    pl.semaphore_wait(barrier, 7)
    for copy in own_in:
        copy.wait()

    def ox(p):
        w_copy(p, 0, 0, 0 if p in FAR else 1, xr).start()
        w_copy(p, 0, 0, 1 if p in FAR else 3, xl).start()

    def oz(p):
        w_copy(p, 0, 0, 3 if p in FAR else 0, zz).start()

    def nc(p):
        w_wait(p, 0, 1, 0)
        w_copy(p, 0, 1, 3, xr).start()
        w_copy(p, 0, 1, 2, xl).start()

    def nr(p):
        w_wait(p, 3, 0, 1)
        w_copy(p, 3, 0, 3, xr).start()

    def nl(p):
        w_wait(p, 1, 1, 2)
        w_copy(p, 1, 1, 3, xl).start()

    def fr(p):
        w_wait(p, 3, 0, 0)
        w_copy(p, 3, 0, 2, xr, 0, 32).start()
        w_copy(p, 3, 0, 3, zz).start()

    def fl(p):
        w_wait(p, 1, 0, 1)
        w_copy(p, 1, 0, 2, xl, 32, 32).start()
        w_copy(p, 1, 0, 3, zz).start()

    def ff(p):
        w_wait(p, 2, 0, 2)
        w_copy(p, 2, 0, 3, zz).start()

    def t00(_):
        small[0].wait()
        small[1].wait()
        first, second = amp_v[:, 0:256], amp_v[:, 256:512]
        stored0 = jnp.full((PAIRS, 256), order[0], jnp.int32) == 0
        stored1 = jnp.full((PAIRS, 256), order[1], jnp.int32) == 1
        mine = pl.multiple_of(col * PAIRS, PAIRS)
        t[pl.ds(mine, PAIRS), 0:256] = jnp.where(stored0, first, second)
        t[pl.ds(mine, PAIRS), 256:512] = jnp.where(stored1, second, first)
        t_copy(0, 0, 0, zn).start()
        t_copy(0, 0, 1, yr).start()
        t_copy(0, 0, 2, yl).start()
        t_copy(0, 0, 7, sib).start()

    def t01(_):
        t_wait(0, 1, 0)
        t_copy(0, 1, 3, yr).start()
        t_copy(0, 1, 4, yl).start()
        t_copy(0, 1, 7, sib).start()

    def t30(_):
        t_wait(3, 0, 1)
        t_copy(3, 0, 5, yr).start()
        t_copy(3, 0, 7, sib).start()

    def t10(_):
        t_wait(1, 0, 2)
        t_copy(1, 0, 7, sib).start()

    def t31(_):
        t_wait(3, 1, 3)
        t_copy(3, 1, 7, sib).start()

    def t11(_):
        t_wait(1, 1, 4)
        t_copy(1, 1, 6, yl).start()
        t_copy(1, 1, 7, sib).start()

    def t20(_):
        t_wait(2, 0, 5)
        t_copy(2, 0, 7, sib).start()

    def t21(_):
        t_wait(2, 1, 6)
        t_copy(2, 1, 7, sib).start()

    def pairs(_):
        for copy in small[2:]:
            copy.wait()
        index = pair_v[...]

        def pick(o, found):
            return jnp.where(index == o, occ[o], found)

        picked = lax.fori_loop(0, occ.shape[0], pick, jnp.zeros(index.shape, jnp.float32), unroll=8)
        pair_row = picked[0:1] + picked[1:2]
        for at in range(0, pair_row.shape[1], 128):
            spread = jnp.broadcast_to(pair_row[:, at : at + 128], (128, 128))
            pe[at : at + 128, :] = spread.T
        for p in range(EARLY, PIECES):
            late_ve[:, (p - EARLY) * STRIP : (p - EARLY + 1) * STRIP] = vir[col * PIECES + p] + vir_row[...]

    def wait_bytes(ref, sem):
        pltpu.make_async_copy(ref, ref, sem).wait()

    def whole(p):
        wait_bytes(w_of(p).at[pl.ds(0, 4 * ROWS)], w_recv.at[p, 3])

    def mul(p):
        if p == 0:
            wait_bytes(t.at[pl.ds(0, 8 * PAIRS)], t_recv.at[7])
        whole(p)
        ve = vir[col * PIECES + p] + vir_row[...]
        ladder_tile(t, w_of(p), pe, ve, done.at[:, pl.ds(p * STRIP, STRIP)])

    steps = dict(
        ox=ox, oz=oz, nc=nc, nr=nr, nl=nl, fr=fr, fl=fl, ff=ff, mul=mul, pairs=pairs,
        t00=t00, t01=t01, t30=t30, t10=t10, t31=t31, t11=t11, t20=t20, t21=t21,
    )
    for name, p in STEPS:
        steps[name](p)
    wait_bytes(t.at[pl.ds(0, 15 * PAIRS)], t_send)
    for p in range(PIECES):
        wait_bytes(w_of(p).at[pl.ds(0, 7 * ROWS)], w_send.at[p])
    for p in range(EARLY, PIECES):
        whole(p)


def finish_kernel(done, t, late, pe, late_ve, out, tail, sem):
    width = EARLY * STRIP
    copies = [pltpu.make_async_copy(done, out.at[:, pl.ds(0, width)], sem.at[0])]
    copies[0].start()
    for k in range(PIECES - EARLY):
        ladder_tile(t, late.at[k], pe, late_ve[:, k * STRIP : (k + 1) * STRIP], tail.at[k])
        copy = pltpu.make_async_copy(
            tail.at[k], out.at[:, pl.ds(width + k * STRIP, STRIP)], sem.at[k + 1]
        )
        copy.start()
        copies.append(copy)
    for copy in copies:
        copy.wait()


def shards(amplitudes, integrals, pair_list, panel_order, occ_energy, vir_energy):
    vmem, hbm = pl.BlockSpec(memory_space=pltpu.VMEM), pl.BlockSpec(memory_space=pltpu.HBM)
    rows, depth, columns = 16 * PAIRS, 8 * ROWS, PIECES * STRIP
    late_count = PIECES - EARLY
    done, t, late, pe, late_ve = pl.pallas_call(
        gather_kernel,
        out_shape=(
            pltpu.VMEM((rows, EARLY * STRIP), jnp.bfloat16),
            pltpu.VMEM((rows, depth), jnp.bfloat16),
            pltpu.VMEM((late_count, depth, STRIP), jnp.bfloat16),
            pltpu.VMEM((rows, 128), jnp.float32),
            pltpu.VMEM((1, late_count * STRIP), jnp.float32),
        ),
        in_specs=[hbm] * 7,
        out_specs=(vmem,) * 5,
        scratch_shapes=[
            pltpu.VMEM((EARLY, depth, STRIP), jnp.bfloat16),
            pltpu.VMEM((PAIRS, depth), jnp.bfloat16),
            pltpu.VMEM((2, rows), jnp.int32),
            pltpu.VMEM((1, vir_energy.shape[0]), jnp.float32),
            pltpu.SMEM((2,), jnp.int32),
            pltpu.SMEM((200,), jnp.float32),
            pltpu.SMEM((512,), jnp.float32),
            pltpu.SemaphoreType.DMA((PIECES,)),
            pltpu.SemaphoreType.DMA((6,)),
            pltpu.SemaphoreType.DMA((PIECES,)),
            pltpu.SemaphoreType.DMA((PIECES, 4)),
            pltpu.SemaphoreType.DMA,
            pltpu.SemaphoreType.DMA((8,)),
        ],
        cost_estimate=pl.CostEstimate(
            flops=2 * rows * depth * EARLY * STRIP, bytes_accessed=4 << 20, transcendentals=0
        ),
        compiler_params=pltpu.CompilerParams(
            collective_id=0, has_side_effects=True, vmem_limit_bytes=32 << 20
        ),
        name="gather",
    )(*(pltpu.with_memory_space_constraint(given, pltpu.HBM) for given in (
        integrals, amplitudes, pair_list, panel_order, occ_energy, vir_energy, vir_energy.reshape(1, -1),
    )))
    return pl.pallas_call(
        finish_kernel,
        out_shape=jax.ShapeDtypeStruct((rows, columns), jnp.bfloat16),
        in_specs=[vmem] * 5,
        out_specs=hbm,
        scratch_shapes=[
            pltpu.VMEM((late_count, rows, STRIP), jnp.bfloat16),
            pltpu.SemaphoreType.DMA((late_count + 1,)),
        ],
        cost_estimate=pl.CostEstimate(
            flops=2 * rows * depth * late_count * STRIP,
            bytes_accessed=2 * rows * columns,
            transcendentals=0,
        ),
        compiler_params=pltpu.CompilerParams(vmem_limit_bytes=32 << 20),
        name="finish",
    )(done, t, late, pe, late_ve)


def solution(mesh):
    placed = (P(("row", "col"), None), P("row", "col"), P(None, "row"), P(), P(), P())
    return jax.shard_map(
        shards, mesh=mesh, in_specs=placed, out_specs=P("row", "col"), check_vma=False
    )
```
